32 devices in a mesh: dp: 2 (over y), expert: 16 (over z, x, core).
Axes of the slice: x: 2, y: 2, z: 4, core: 2. Of those that a mesh axis runs over, the one named last changes fastest.
Arguments:
- attention: bfloat16 [4096, 1536], P(('dp', 'expert')), may hold values from -6 to 6
- residual: bfloat16 [4096, 1536], P(('dp', 'expert')), may hold values from -6 to 6
- out_weight: bfloat16 [1536, 1536], P(('dp', 'expert')), may hold values from -0.15625 to 0.15625
- gate_weight: bfloat16 [16, 1536, 512], P('expert', 'dp'), may hold values from -0.15625 to 0.15625
- up_weight: bfloat16 [16, 1536, 512], P('expert', 'dp'), may hold values from -0.15625 to 0.15625
- down_weight: bfloat16 [16, 512, 1536], P('expert'), may hold values from -0.25 to 0.25
- routes: int32 [4096, 8], P(('dp', 'expert')), may hold values from 0 to 15, all different within a row; in each aligned block of 128 rows (0 to 127, 128 to 255, ...) at most 80 rows name the same one
- router_scores: float32 [4096, 8], P(('dp', 'expert')), may hold values from 0.05 to 1
- norm_gain: float32 [1536], replicated, may hold values from 0.5 to 1.5
Outputs:
- normed: bfloat16 [4096, 1536], P(('dp', 'expert'))
The draws below stay inside these ranges and needn't reach their ends.
Inputs may be any that keep to these rules, and one draw needn't show every extreme that they name: `routes`: in each aligned block of 128 rows (the rows of one device) no expert is named by more than 80 rows, a bound that some block reaches; a row names 8 different experts.
All inputs are finite; a program needn't handle non-finite values.
Results may differ from the reference program's by a relative error of at most 0.0053.
Values may be sent and summed in bfloat16 or wider, within the bound.
No kernel may reach another device: no remote copies, remote signals or barrier semaphores. Data moves between devices by JAX's collectives and lax.ppermute only.
A program may use at most 64 MiB of HBM per device.

```python
import math
import jax
import jax.numpy as jnp
import numpy as np
from jax import lax

D = 1536
FFH = 512
TOPK = 8
TOK_DEV = 128
EXPERTS = 16
CAP = 80
TOKENS = 4096


def block_levels(rng, extent, split, least, largest):
    def one(dim, parts):
        draws = jax.random.uniform(jax.random.fold_in(jax.random.fold_in(rng, 6), dim), (parts,), jnp.float32, least / len(split), largest / len(split))
        return jnp.repeat(jnp.exp(draws), extent[dim] // parts).reshape((-1,) + (1,) * (len(extent) - dim - 1))

    level = one(*split[0])
    for cut in split[1:]:
        level = level * one(*cut)
    return level


def routed_block(rng, own, number, rows, amount, top, bound, lean):
    order = jax.random.permutation(rng, amount)
    heavy_load, common = shares(amount, rows * top, bound, lean, True), shares(amount, rows * top, bound, lean, False)
    places = jnp.arange(amount)

    def named(lengths, offset_by):
        used = int((lengths > 0).sum())
        fixed = max(1, used // 4)
        shifted = fixed + (places - fixed + offset_by * (used - fixed)) % max(1, amount - fixed)
        return jnp.zeros((amount,), jnp.int32).at[order[jnp.where(places < fixed, places, shifted)]].set(jnp.asarray(lengths, jnp.int32))

    lengths = jnp.where(number % 4 == 0, named(heavy_load, number // 4), named(common, number - number // 4 - 1))
    mixed = jax.random.permutation(jax.random.fold_in(own, 3), amount)
    donor, taker = mixed[0:amount // 2 * 2:2], mixed[1:amount // 2 * 2:2]
    room = jnp.minimum(lengths[donor] - 1, bound - lengths[taker]) // 2
    room = jnp.where((donor == order[0]) | (taker == order[0]) | (lengths[taker] == 0), 0, jnp.maximum(room, 0))
    shifted = jax.random.randint(jax.random.fold_in(own, 4), (amount // 2,), 0, 1 << 20) % (room + 1)
    lengths = lengths.at[donor].add(-shifted).at[taker].add(shifted)
    members = jnp.searchsorted(jnp.cumsum(lengths), jnp.arange(rows * top), side="right").astype(jnp.int32)
    grid = members.reshape(top, rows).T
    grid = grid[jax.random.permutation(jax.random.fold_in(own, 1), rows)]
    offset_by = jax.random.randint(jax.random.fold_in(own, 2), (rows, 1), 0, top)
    return jnp.take_along_axis(grid, (jnp.arange(top)[None, :] + offset_by) % top, axis=1)


def shares(amount, total, limit, skew, full):
    weights = [(1 << 20) // math.isqrt(grade ** skew) + 1 for grade in range(1, amount + 1)]
    largest = limit if full else min(limit, max(-(-total // amount), total * weights[0] // sum(weights)))
    least = 1 if total - largest >= amount - 1 else 0
    counts, surplus = [largest] + [least] * (amount - 1), total - largest - least * (amount - 1)
    while surplus > 0:
        movable = [i for i in range(1, amount) if counts[i] < largest] or [i for i in range(1, amount) if counts[i] < limit]
        whole, budget = sum([weights[i] for i in movable]), surplus
        for i in movable:
            addition = min(limit - counts[i], max(1, budget * weights[i] // whole), surplus)
            counts[i] = counts[i] + addition
            surplus = surplus - addition
    return np.array(counts)


def bell_draw(rng, dims, scale, limit, pieces=(), held_as=jnp.bfloat16):
    factor_of = block_levels(rng, dims, pieces, -0.22, 0.18) if pieces else 1.0
    result = jax.random.normal(rng, dims, jnp.float32) * scale * factor_of
    return jnp.minimum(jnp.maximum(result, -limit), limit).astype(held_as)


def setup_inputs(seed: int = 0) -> dict:
    streams_of = jax.random.split(jax.random.key(seed), 10)
    attention = bell_draw(streams_of[0], (TOKENS, D), 1.0, 6.0, ((0, 32),))
    residual = bell_draw(streams_of[1], (TOKENS, D), 1.0, 6.0, ((0, 32),))
    out_weight = bell_draw(streams_of[2], (D, D), D ** -0.5, 0.15625, ((0, 32),))
    gate_weight = bell_draw(streams_of[3], (EXPERTS, D, FFH), D ** -0.5, 0.15625, ((0, 16), (1, 2)))
    up_weight = bell_draw(streams_of[4], (EXPERTS, D, FFH), D ** -0.5, 0.15625, ((0, 16), (1, 2)))
    down_weight = bell_draw(streams_of[5], (EXPERTS, FFH, D), FFH ** -0.5, 0.25, ((0, 16),))
    routes_keys = jax.random.split(jax.random.fold_in(streams_of[6], 1), TOKENS // TOK_DEV)
    routes_turns = jax.random.permutation(jax.random.fold_in(streams_of[6], 3), TOKENS // TOK_DEV)
    routes = jax.vmap(lambda own, number: routed_block(jax.random.fold_in(streams_of[6], 2), own, number, TOK_DEV, EXPERTS, TOPK, CAP, 2))(routes_keys, routes_turns).reshape((TOKENS, TOPK))
    router_scores = jnp.clip(jnp.exp(math.log(1.0) - 2.9957323 * jax.random.uniform(streams_of[7], (TOKENS, TOPK), jnp.float32) ** block_levels(streams_of[7], (TOKENS, TOPK), ((0, 32),), -0.2, 0.2)), 0.05, 1.0)
    norm_gain = jnp.clip(1.0 + 0.1 * jax.random.normal(streams_of[8], (D,), jnp.float32), 0.5, 1.5)
    return {"attention": attention, "residual": residual, "out_weight": out_weight, "gate_weight": gate_weight, "up_weight": up_weight, "down_weight": down_weight, "routes": routes, "router_scores": router_scores, "norm_gain": norm_gain}


def reference(attention, residual, out_weight, gate_weight, up_weight, down_weight, routes, router_scores, norm_gain):
    projected = jnp.dot(attention, out_weight, preferred_element_type=jnp.float32)
    stream = (residual.astype(jnp.float32) + projected).astype(jnp.bfloat16)
    groups = TOKENS // TOK_DEV
    pairs = routes.reshape(groups, TOK_DEV * TOPK).astype(jnp.int32)
    onehot = (pairs[:, :, None] == jnp.arange(EXPERTS, dtype=jnp.int32)[None, None, :]).astype(jnp.int32)
    earlier = jnp.cumsum(onehot, axis=1) - onehot
    position = lax.optimization_barrier(jnp.sum(earlier * onehot, axis=2)).astype(jnp.int32)
    group_index = jnp.arange(groups, dtype=jnp.int32)[:, None]
    target = pairs * (groups * CAP) + group_index * CAP + position
    token_index = group_index * TOK_DEV + jnp.arange(TOK_DEV * TOPK, dtype=jnp.int32)[None, :] // TOPK
    combine = router_scores / lax.optimization_barrier(jnp.sum(router_scores, axis=1, keepdims=True))
    table = jnp.full((EXPERTS * groups * CAP,), TOKENS, jnp.int32).at[target.reshape(-1)].set(token_index.reshape(-1))
    table = table.reshape(EXPERTS, groups * CAP)
    weight_table = jnp.zeros((EXPERTS * groups * CAP,), jnp.float32).at[target.reshape(-1)].set(combine.reshape(-1))
    weight_table = weight_table.reshape(EXPERTS, groups * CAP)
    padded = jnp.concatenate([stream, jnp.zeros((1, D), jnp.bfloat16)], axis=0)

    def one_expert(mixture, items):
        indices, weights, gate_mat, up_mat, down_mat = items
        rows_in = padded[indices]
        gate_act = jnp.dot(rows_in, gate_mat, preferred_element_type=jnp.float32)
        up_act = jnp.dot(rows_in, up_mat, preferred_element_type=jnp.float32)
        expert_hidden = (jax.nn.silu(gate_act) * up_act).astype(jnp.bfloat16)
        expert_out = jnp.dot(expert_hidden, down_mat, preferred_element_type=jnp.float32).astype(jnp.bfloat16)
        mixture = mixture.at[indices].add(weights[:, None] * expert_out.astype(jnp.float32))
        return (mixture, None)
    start_mix = jnp.zeros((TOKENS + 1, D), jnp.float32)
    mixture, unused = lax.scan(one_expert, start_mix, (table, weight_table, gate_weight, up_weight, down_weight))
    total = stream.astype(jnp.float32) + mixture[:TOKENS]
    scale = lax.rsqrt(lax.optimization_barrier(jnp.mean(total * total, axis=1, keepdims=True)) + 1e-06)
    return (total * scale * norm_gain[None, :]).astype(jnp.bfloat16)
```

```python
import functools

import jax
import jax.numpy as jnp
import numpy as np
from jax import lax
from jax.experimental import pallas as pl
from jax.experimental.pallas import tpu as pltpu
from jax.sharding import PartitionSpec as P

BF16 = jnp.bfloat16
F32 = jnp.float32


def expert_kernel(place_ref, *refs):
    own_a, own_b, near_a, near_b, gate_a, gate_b, up_a, up_b, down, own_mix, near_mix, own_out, near_out = refs
    expert = place_ref[1]

    def weight(ref):
        lane = lax.broadcasted_iota(jnp.int32, ref.shape, 1)
        return jnp.sum(jnp.where(lane == expert, ref[...], 0.0), axis=1, keepdims=True)

    first = jnp.concatenate([own_a[...], near_a[...]], axis=0)
    second = jnp.concatenate([own_b[...], near_b[...]], axis=0)
    dot = functools.partial(jnp.dot, preferred_element_type=F32)
    gate_act = dot(first, gate_a[...]) + dot(second, gate_b[...])
    up_act = dot(first, up_a[...]) + dot(second, up_b[...])
    hidden = (jax.nn.silu(gate_act) * up_act).astype(BF16)
    result = dot(hidden, down[...])
    rows = own_a.shape[0]
    own_out[...] = result[:rows] * weight(own_mix)
    near_out[...] = (result[rows:] * weight(near_mix)).astype(BF16)


def run_expert(place, block, weights, mix):
    rows = mix.shape[0] // 2
    half = weights[0].shape[0]
    width = weights[4].shape[1]

    def picked(shape, near):
        if near:
            return pl.BlockSpec(shape, lambda i, place: (1 - place[0], 0))
        return pl.BlockSpec(shape, lambda i, place: (place[0], 0))

    def whole(array):
        return pl.BlockSpec(array.shape, lambda i, place: (0, 0))

    if len(block) == 2:
        first, second = block
        tokens = (first, second, first, second)
        token_specs = [picked((rows, half), near) for near in (False, False, True, True)]
    else:
        tokens = block
        token_specs = [whole(array) for array in block]
    mix_specs = [picked((rows, mix.shape[1]), False), picked((rows, mix.shape[1]), True)]
    flops = 2 * 2 * rows * (2 * half * 2 * weights[0].shape[1] + weights[4].shape[0] * width)
    return pl.pallas_call(
        expert_kernel,
        grid_spec=pltpu.PrefetchScalarGridSpec(
            num_scalar_prefetch=1,
            grid=(1,),
            in_specs=token_specs + [whole(array) for array in weights] + mix_specs,
            out_specs=[pl.BlockSpec((rows, width), lambda i, place: (0, 0))] * 2,
        ),
        out_shape=[
            jax.ShapeDtypeStruct((rows, width), F32),
            jax.ShapeDtypeStruct((rows, width), BF16),
        ],
        compiler_params=pltpu.CompilerParams(vmem_limit_bytes=32 * 1024 * 1024),
        cost_estimate=pl.CostEstimate(flops=flops, bytes_accessed=8 * 1024 * 1024, transcendentals=0),
    )(place, *tokens, *weights, mix, mix)


def body(
    attention,
    residual,
    out_weight,
    gate_weight,
    up_weight,
    down_weight,
    routes,
    router_scores,
    norm_gain,
):
    token_count, width = attention.shape
    half = width // 2
    groups = lax.axis_size("dp")
    peers = lax.axis_size("expert")
    chips = peers // 2
    far = chips // 2
    group = lax.axis_index("dp")
    expert = lax.axis_index("expert")
    core = expert % 2
    ring = list(range(0, chips, 2)) + list(range(chips - 1, 0, -2))
    ring_of = np.argsort(np.array(ring))
    at = jnp.asarray(ring_of, jnp.int32)[expert // 2]
    pair_at = jnp.asarray(ring, jnp.int32)
    forth = [(2 * ring[k] + c, 2 * ring[(k + 1) % chips] + c) for k in range(chips) for c in range(2)]
    back = [(b, a) for a, b in forth]
    across = [(e, e ^ 1) for e in range(peers)]

    def swap(x):
        return lax.ppermute(x, "expert", across)

    def go(x):
        return lax.ppermute(x, "expert", forth)

    def come(x):
        return lax.ppermute(x, "expert", back)

    def columns(x, which):
        return lax.dynamic_slice(x, (0, which * half), (x.shape[0], half))

    def paired(mine, other):
        return jnp.where(core == 0, jnp.concatenate([mine, other], 0), jnp.concatenate([other, mine], 0))

    combine = router_scores / jnp.sum(router_scores, axis=1, keepdims=True)
    named = routes[:, :, None] == jnp.arange(peers, dtype=jnp.int32)[None, None, :]
    dense = jnp.sum(jnp.where(named, combine[:, :, None], 0.0), axis=1)
    mix_all = lax.all_gather(dense, "expert", axis=0, tiled=True).reshape(chips, 2 * token_count, peers)

    tokens = paired(attention, swap(attention))
    base = paired(columns(residual, core), swap(columns(residual, 1 - core)))
    if groups == 2:
        mine = jnp.concatenate([columns(out_weight, core), swap(columns(out_weight, 1 - core))], axis=0)
        other = lax.ppermute(mine, "dp", [(0, 1), (1, 0)])
        parts = [(mine, 0, 0), (other, 0, 1)]
        mine_f = mine_b = mine
        other_f = other_b = other
        for step in range(1, far + 1):
            mine_f = go(mine_f)
            parts.append((mine_f, -step, 0))
            other_b = come(other_b)
            parts.append((other_b, step, 1))
            if step < far:
                mine_b = come(mine_b)
                parts.append((mine_b, step, 0))
                other_f = go(other_f)
                parts.append((other_f, -step, 1))
        rows = out_weight.shape[0]
        starts = []
        for _, offset, other_group in parts:
            pair = pair_at[(at + offset) % chips]
            of_group = (group + other_group) % 2
            for c in (core, 1 - core):
                starts.append(((of_group * chips + pair) * 2 + c) * rows)
        order = (jnp.stack(starts)[:, None] + jnp.arange(rows, dtype=jnp.int32)[None, :]).reshape(-1)
        place_matrix = (jnp.arange(width, dtype=jnp.int32)[:, None] == order[None, :]).astype(BF16)
        tokens = jnp.dot(tokens, place_matrix, preferred_element_type=F32).astype(BF16)
        half_weight = jnp.concatenate([p[0] for p in parts], axis=0)
        near_first = core == group
        flip = [(0, 1), (1, 0)]

        def halves(x):
            x = x[0]
            y = lax.ppermute(x, "dp", flip)
            return jnp.where(near_first, x, y), jnp.where(near_first, y, x)

    else:
        half_weight = columns(lax.all_gather(out_weight, ("dp", "expert"), axis=0, tiled=True), core)

        def halves(x):
            x = lax.all_gather(x, "dp", axis=1, tiled=True)[0]
            return (
                lax.dynamic_slice(x, (core * half, 0), (half, x.shape[1])),
                lax.dynamic_slice(x, ((1 - core) * half, 0), (half, x.shape[1])),
            )

    projected = jnp.dot(tokens, half_weight, preferred_element_type=F32)
    stream = (base.astype(F32) + projected).astype(BF16)

    gate = halves(gate_weight)
    up = halves(up_weight)
    weights = (*gate, *up, down_weight[0])
    place = jnp.stack([core, expert]).astype(jnp.int32)

    def experts(block, offset):
        return run_expert(place, block, weights, mix_all[pair_at[(at + offset) % chips]])

    out = {}
    stream_near = swap(stream)
    out[0] = experts((stream, stream_near), 0)
    f = b = stream
    for step in range(1, far):
        f, b = go(f), come(b)
        out[-step] = experts((f, swap(f)), -step)
        out[step] = experts((b, swap(b)), step)
    f = go(lax.dynamic_slice(f, (core * token_count, 0), (token_count, half)))
    b = come(lax.dynamic_slice(b, ((1 - core) * token_count, 0), (token_count, half)))
    out[far] = experts((f, swap(b), b, swap(f)), far)

    shared = {offset: (own, swap(near)) for offset, (own, near) in out.items()}
    cut = token_count // 2

    def term(offset, part):
        own, near = shared[offset]
        rows = slice(part * cut, (part + 1) * cut)
        return own[rows] + near[rows].astype(F32)

    def chain(move, sign, part, distance):
        total = term(distance if distance == far else sign * distance, part).astype(BF16)
        total = move(total)
        for left in range(distance - 1, 0, -1):
            total = move((term(sign * left, part) + total.astype(F32)).astype(BF16))
        return total.astype(F32)

    mixture = jnp.concatenate(
        [
            term(0, 0) + chain(go, 1, 0, far) + chain(come, -1, 0, far - 1),
            term(0, 1) + chain(come, -1, 1, far) + chain(go, 1, 1, far - 1),
        ],
        axis=0,
    )
    own_rows = lax.dynamic_slice(stream, (core * token_count, 0), (token_count, half))
    near_rows = lax.dynamic_slice(stream_near, (core * token_count, 0), (token_count, half))
    whole_rows = jnp.where(
        core == 0,
        jnp.concatenate([own_rows, near_rows], axis=1),
        jnp.concatenate([near_rows, own_rows], axis=1),
    )
    total = whole_rows.astype(F32) + mixture
    scale = lax.rsqrt(jnp.mean(total * total, axis=1, keepdims=True) + 1e-06)
    return (total * scale * norm_gain[None, :]).astype(BF16)


def solution(mesh):
    in_specs = (
        P(("dp", "expert"), None),
        P(("dp", "expert"), None),
        P(("dp", "expert"), None),
        P("expert", "dp", None),
        P("expert", "dp", None),
        P("expert", None, None),
        P(("dp", "expert"), None),
        P(("dp", "expert"), None),
        P(),
    )
    out_specs = P(("dp", "expert"), None)
    return jax.shard_map(body, mesh=mesh, in_specs=in_specs, out_specs=out_specs, check_vma=False)
```

```python
import functools

import jax
import jax.numpy as jnp
from jax import lax
from jax.experimental import pallas as pl
from jax.experimental.pallas import tpu as pltpu
from jax.sharding import PartitionSpec as P

BF16 = jnp.bfloat16
F32 = jnp.float32
VMEM = pl.BlockSpec(memory_space=pltpu.VMEM)
SMEM = pl.BlockSpec(memory_space=pltpu.SMEM)
PIECES = 3
dot = functools.partial(jnp.dot, preferred_element_type=F32)


def ring_order(chips):
    return list(range(0, chips, 2)) + list(range(chips - 1, 0, -2))


def call(kernel, out_shape, *args, scratch=(), flops=0, name=None):
    return pl.pallas_call(
        kernel,
        in_specs=[SMEM] + [VMEM] * (len(args) - 1),
        out_specs=jax.tree.map(lambda _: VMEM, out_shape),
        out_shape=out_shape,
        scratch_shapes=list(scratch),
        compiler_params=pltpu.CompilerParams(vmem_limit_bytes=32 * 1024 * 1024),
        cost_estimate=pl.CostEstimate(flops=flops, bytes_accessed=4 * 1024 * 1024, transcendentals=0),
        name=name,
    )(*args)


def stream_kernel(layout, place, att, att_near, res, res_near, routes, scores, *refs):
    *blocks, out, full, tokens = refs
    core, expert, group = place[0], place[1], place[2]
    rows, width = att.shape
    half = width // 2
    extra = out.shape[0] - 2 * rows
    mine = pl.ds(pl.multiple_of(core * half, 128), half)
    own_rows = pl.ds(pl.multiple_of(core * rows, 16), rows)
    near_rows = pl.ds(pl.multiple_of((1 - core) * rows, 16), rows)
    tokens[own_rows, :] = att[...]
    tokens[near_rows, :] = att_near[...]
    if layout is None:
        full[...] = blocks[0][:, mine]
    else:
        chips, where = layout
        pair = lax.shift_right_logical(expert, 1)
        down = (pair & 1) == 1
        at = jnp.where(down, chips - lax.shift_right_logical(pair + 1, 1), lax.shift_right_logical(pair, 1))
        for block, (offset, other) in zip(blocks, where, strict=True):
            spot = lax.rem(at + (offset + chips), chips)
            source = jnp.where(spot < chips // 2, 2 * spot, 2 * (chips - spot) - 1)
            of_group = group if other == 0 else 1 - group
            depth = block.shape[0] // 2
            for index, c in enumerate((core, 1 - core)):
                start = ((of_group * chips + source) * 2 + c) * depth
                full[pl.ds(pl.multiple_of(start, 16), depth), :] = block[index * depth : (index + 1) * depth, :]
    projected = dot(tokens[...], full[...])
    for c in range(2):
        at_rows = slice(c * (rows + extra), c * (rows + extra) + rows)
        part = projected[c * rows : (c + 1) * rows]

        @pl.when(core == c)
        def _(at_rows=at_rows, part=part):
            out[at_rows, :] = (res[:, mine].astype(F32) + part).astype(BF16)

        @pl.when(core != c)
        def _(at_rows=at_rows, part=part):
            out[at_rows, :] = (res_near[:, mine].astype(F32) + part).astype(BF16)

    combine = scores[...] / jnp.sum(scores[...], axis=0, keepdims=True)
    named = lax.broadcasted_iota(jnp.int32, (extra, rows), 0)
    left = jnp.zeros((extra, rows), F32)
    for k in range(routes.shape[0]):
        left = left + jnp.where(routes[k : k + 1, :] == named, combine[k : k + 1, :], 0.0)
    for piece in range(PIECES):
        value = left.astype(BF16)
        out[rows : rows + extra, piece * rows : (piece + 1) * rows] = value
        left = left - value.astype(F32)


def expert_kernel(parts, place, *refs):
    *tokens, gate_a, gate_b, up_a, up_b, down, own_out, near_out = refs
    core, expert, group = place[0], place[1], place[2]
    rows = own_out.shape[0]

    def split(arrays):
        extra = arrays[0].shape[0] - rows if len(arrays) == 2 else arrays[0].shape[0] - 2 * rows
        if len(arrays) == 2:
            return arrays[0][:rows, :], arrays[1][extra:, :], arrays[0][rows:, : PIECES * rows]
        whole = arrays[0]
        return whole[:rows, :], whole[rows + extra :, :], whole[rows : rows + extra, : PIECES * rows]

    own = split(tokens[:parts])
    near = split(tokens[parts:])
    same = core == group
    first = jnp.concatenate([jnp.where(same, own[c], near[c]) for c in range(2)], axis=0)
    second = jnp.concatenate([jnp.where(same, near[c], own[c]) for c in range(2)], axis=0)
    gate_act = dot(first, gate_a[...]) + dot(second, gate_b[...])
    up_act = dot(first, up_a[...]) + dot(second, up_b[...])
    hidden = (jax.nn.silu(gate_act) * up_act).astype(BF16)
    result = dot(hidden, down[...])

    def weight(pieces):
        pieces = pieces.astype(F32)
        total = pieces[:, :rows]
        for piece in range(1, PIECES):
            total = total + pieces[:, piece * rows : (piece + 1) * rows]
        at_expert = lax.broadcasted_iota(jnp.int32, total.shape, 0) == expert
        line = jnp.sum(jnp.where(at_expert, total, 0.0), axis=0, keepdims=True)
        square = (rows, rows)
        diagonal = lax.broadcasted_iota(jnp.int32, square, 0) == lax.broadcasted_iota(jnp.int32, square, 1)
        return jnp.sum(jnp.where(diagonal, jnp.broadcast_to(line, square), 0.0), axis=1, keepdims=True)

    by_core = (jnp.where(core == 0, own[2], near[2]), jnp.where(core == 0, near[2], own[2]))
    for c in range(2):
        weighted = result[c * rows : (c + 1) * rows] * weight(by_core[c])

        @pl.when(core == c)
        def _(weighted=weighted):
            own_out[...] = weighted

        @pl.when(core != c)
        def _(weighted=weighted):
            near_out[...] = weighted.astype(BF16)


def final_kernel(place, own, near, mine, shared, first_a, first_b, second_a, second_b, gain, out):
    core = place[0]
    rows, width = out.shape
    extra = own.shape[0] - 2 * rows
    half = width // 2
    cut = rows // 2
    at_rows = pl.ds(pl.multiple_of(core * (rows + extra), 16), rows)
    own_half, near_half = own[at_rows, :].astype(F32), near[at_rows, :].astype(F32)
    stream = jnp.concatenate(
        [jnp.where(core == 0, own_half, near_half), jnp.where(core == 0, near_half, own_half)], axis=1
    )
    base = stream + mine[...] + shared[...].astype(F32)
    sums = ((first_a, first_b), (second_a, second_b))
    for index, (a, b) in enumerate(sums):
        total = base[index * cut : (index + 1) * cut] + (a[...].astype(F32) + b[...].astype(F32))
        scale = lax.rsqrt(jnp.sum(total * total, axis=1, keepdims=True) / width + 1e-06)
        out[index * cut : (index + 1) * cut, :] = (total * scale * gain[...]).astype(BF16)


def body(
    attention,
    residual,
    out_weight,
    gate_weight,
    up_weight,
    down_weight,
    routes,
    router_scores,
    norm_gain,
):
    token_count, width = attention.shape
    half = width // 2
    groups = lax.axis_size("dp")
    peers = lax.axis_size("expert")
    chips = peers // 2
    far = chips // 2
    ring = ring_order(chips)
    forth = [(2 * ring[k] + c, 2 * ring[(k + 1) % chips] + c) for k in range(chips) for c in range(2)]
    back = [(b, a) for a, b in forth]
    across = [(e, e ^ 1) for e in range(peers)]
    group = lax.axis_index("dp")
    expert = lax.axis_index("expert")
    core = expert & 1
    place = jnp.stack([core, expert, group if groups == 2 else jnp.zeros_like(group)]).astype(jnp.int32)

    def swap(x):
        return lax.ppermute(x, "expert", across)

    def go(x):
        return lax.ppermute(x, "expert", forth)

    def come(x):
        return lax.ppermute(x, "expert", back)

    if groups == 2:
        flip = [(0, 1), (1, 0)]

        def columns(which):
            return lax.dynamic_slice(
                out_weight, (0, which * half), (out_weight.shape[0], half), allow_negative_indices=False
            )

        mine = jnp.concatenate([columns(core), swap(columns(1 - core))], axis=0)
        other = lax.ppermute(mine, "dp", flip)
        blocks, layout = [mine, other], [(0, 0), (0, 1)]
        mine_f = mine_b = mine
        other_f = other_b = other
        for step in range(1, far + 1):
            mine_f, other_b = go(mine_f), come(other_b)
            blocks += [mine_f, other_b]
            layout += [(-step, 0), (step, 1)]
            if step < far:
                mine_b, other_f = come(mine_b), go(other_f)
                blocks += [mine_b, other_f]
                layout += [(step, 0), (-step, 1)]
        layout = (chips, layout)
        gate, up = gate_weight[0], up_weight[0]
        weights = (gate, lax.ppermute(gate, "dp", flip), up, lax.ppermute(up, "dp", flip), down_weight[0])
    else:
        blocks, layout = [lax.all_gather(out_weight, ("dp", "expert"), axis=0, tiled=True)], None
        gate = lax.all_gather(gate_weight, "dp", axis=1, tiled=True)[0]
        up = lax.all_gather(up_weight, "dp", axis=1, tiled=True)[0]
        weights = (gate[:half], gate[half:], up[:half], up[half:], down_weight[0])

    extra = -(-peers // 16) * 16
    block_rows = 2 * token_count + extra
    stream = call(
        functools.partial(stream_kernel, layout),
        jax.ShapeDtypeStruct((block_rows, half), BF16),
        place,
        attention,
        swap(attention),
        residual,
        swap(residual),
        routes.T,
        router_scores.T,
        *blocks,
        scratch=[pltpu.VMEM((width, half), BF16), pltpu.VMEM((2 * token_count, width), BF16)],
        flops=4 * token_count * width * half,
        name="stream",
    )

    def experts(*tokens):
        hidden = weights[0].shape[1]
        return call(
            functools.partial(expert_kernel, len(tokens) // 2),
            [
                jax.ShapeDtypeStruct((token_count, width), F32),
                jax.ShapeDtypeStruct((token_count, width), BF16),
            ],
            place,
            *tokens,
            *weights,
            flops=4 * token_count * 3 * width * hidden,
            name="experts",
        )

    out = {}
    stream_near = swap(stream)
    out[0] = experts(stream, stream_near)
    f = b = stream
    for step in range(1, far):
        f, b = go(f), come(b)
        out[-step] = experts(f, swap(f))
        out[step] = experts(b, swap(b))
    f, b = go(f[: token_count + extra]), come(b[token_count:])
    out[far] = experts(f, b, swap(f), swap(b))

    shared = {offset: (own, swap(near)) for offset, (own, near) in out.items()}
    cut = token_count // 2

    def term(offset, part):
        own, near = shared[offset]
        rows = slice(part * cut, (part + 1) * cut)
        return own[rows] + near[rows].astype(F32)

    def chain(move, sign, part, distance):
        total = move(term(distance if distance == far else sign * distance, part).astype(BF16))
        for left in range(distance - 1, 0, -1):
            total = move((term(sign * left, part) + total.astype(F32)).astype(BF16))
        return total

    return call(
        final_kernel,
        jax.ShapeDtypeStruct((token_count, width), BF16),
        place,
        stream,
        stream_near,
        *shared[0],
        chain(go, 1, 0, far),
        chain(come, -1, 0, far - 1),
        chain(go, 1, 1, far - 1),
        chain(come, -1, 1, far),
        norm_gain[None, :],
        name="final",
    )


def solution(mesh):
    in_specs = (
        P(("dp", "expert"), None),
        P(("dp", "expert"), None),
        P(("dp", "expert"), None),
        P("expert", "dp", None),
        P("expert", "dp", None),
        P("expert", None, None),
        P(("dp", "expert"), None),
        P(("dp", "expert"), None),
        P(),
    )
    out_specs = P(("dp", "expert"), None)
    return jax.shard_map(body, mesh=mesh, in_specs=in_specs, out_specs=out_specs, check_vma=False)
```

```python
import functools

import jax
import jax.numpy as jnp
from jax import lax
from jax.experimental import pallas as pl
from jax.experimental.pallas import tpu as pltpu
from jax.sharding import PartitionSpec as P

BF16 = jnp.bfloat16
F32 = jnp.float32
VMEM = pl.BlockSpec(memory_space=pltpu.VMEM)
SMEM = pl.BlockSpec(memory_space=pltpu.SMEM)
PIECES = 3
dot = functools.partial(jnp.dot, preferred_element_type=F32)


def ring_order(chips):
    return list(range(0, chips, 2)) + list(range(chips - 1, 0, -2))


def together(*arrays):
    return lax.optimization_barrier(arrays)


def call(kernel, out_shape, *args, scratch=(), flops=0, name=None):
    return pl.pallas_call(
        kernel,
        in_specs=[SMEM] + [VMEM] * (len(args) - 1),
        out_specs=jax.tree.map(lambda _: VMEM, out_shape),
        out_shape=out_shape,
        scratch_shapes=list(scratch),
        compiler_params=pltpu.CompilerParams(vmem_limit_bytes=32 * 1024 * 1024),
        cost_estimate=pl.CostEstimate(flops=flops, bytes_accessed=4 * 1024 * 1024, transcendentals=0),
        name=name,
    )(*args)


def prepare_kernel(place, att, att_near, res, res_near, routes, scores, tokens, base):
    core = place[0]
    rows, width = att.shape
    half = width // 2
    extra = base.shape[0] - 2 * rows
    mine = pl.ds(pl.multiple_of(core * half, 128), half)
    for c in range(2):
        at_rows = slice(c * (rows + extra), c * (rows + extra) + rows)

        @pl.when(core == c)
        def _(c=c, at_rows=at_rows):
            tokens[c * rows : (c + 1) * rows, :] = att[...]
            base[at_rows, :] = res[:, mine]

        @pl.when(core != c)
        def _(c=c, at_rows=at_rows):
            tokens[c * rows : (c + 1) * rows, :] = att_near[...]
            base[at_rows, :] = res_near[:, mine]

    combine = scores[...] / jnp.sum(scores[...], axis=0, keepdims=True)
    named = lax.broadcasted_iota(jnp.int32, (extra, rows), 0)
    left = jnp.zeros((extra, rows), F32)
    for k in range(routes.shape[0]):
        left = left + jnp.where(routes[k : k + 1, :] == named, combine[k : k + 1, :], 0.0)
    base[rows : rows + extra, :] = jnp.zeros((extra, half), BF16)
    for piece in range(PIECES):
        value = left.astype(BF16)
        base[rows : rows + extra, piece * rows : (piece + 1) * rows] = value
        left = left - value.astype(F32)


def stream_kernel(layout, place, tokens, base, *refs):
    *blocks, out, full = refs
    core, expert, group = place[0], place[1], place[2]
    rows, width = tokens.shape[0] // 2, tokens.shape[1]
    half = width // 2
    extra = out.shape[0] - 2 * rows
    if layout is None:
        full[...] = blocks[0][:, pl.ds(pl.multiple_of(core * half, 128), half)]
    else:
        chips, where = layout
        depth = blocks[0].shape[0] // 2
        pair = lax.shift_right_logical(expert, 1)
        down = (pair & 1) == 1
        at = jnp.where(down, chips - lax.shift_right_logical(pair + 1, 1), lax.shift_right_logical(pair, 1))
        for block, (offset, other) in zip(blocks, where, strict=True):
            spot = lax.rem(at + (offset + chips), chips)
            source = jnp.where(spot < chips // 2, 2 * spot, 2 * (chips - spot) - 1)
            of_group = group if other == 0 else 1 - group
            sides = (core, 1 - core)
            if block.shape[0] == depth:
                sides = sides[:1] if offset < 0 else sides[1:]
            for index, c in enumerate(sides):
                start = ((of_group * chips + source) * 2 + c) * depth
                full[pl.ds(pl.multiple_of(start, 16), depth), :] = block[index * depth : (index + 1) * depth, :]
    projected = dot(tokens[...], full[...])
    out[rows : rows + extra, :] = base[rows : rows + extra, :]
    for c in range(2):
        at_rows = slice(c * (rows + extra), c * (rows + extra) + rows)
        out[at_rows, :] = (base[at_rows, :].astype(F32) + projected[c * rows : (c + 1) * rows]).astype(BF16)


def expert_kernel(parts, place, *refs):
    *tokens, gate_a, gate_b, up_a, up_b, down, own_out, near_out = refs
    core, expert, group = place[0], place[1], place[2]
    rows = own_out.shape[0]

    def split(arrays):
        extra = arrays[0].shape[0] - rows if len(arrays) == 2 else arrays[0].shape[0] - 2 * rows
        if len(arrays) == 2:
            return arrays[0][:rows, :], arrays[1][extra:, :], arrays[0][rows:, : PIECES * rows]
        whole = arrays[0]
        return whole[:rows, :], whole[rows + extra :, :], whole[rows : rows + extra, : PIECES * rows]

    own = split(tokens[:parts])
    near = split(tokens[parts:])
    same = core == group
    first = jnp.concatenate([jnp.where(same, own[c], near[c]) for c in range(2)], axis=0)
    second = jnp.concatenate([jnp.where(same, near[c], own[c]) for c in range(2)], axis=0)
    gate_act = dot(first, gate_a[...]) + dot(second, gate_b[...])
    up_act = dot(first, up_a[...]) + dot(second, up_b[...])
    hidden = (jax.nn.silu(gate_act) * up_act).astype(BF16)
    result = dot(hidden, down[...])

    def weight(pieces):
        pieces = pieces.astype(F32)
        total = pieces[:, :rows]
        for piece in range(1, PIECES):
            total = total + pieces[:, piece * rows : (piece + 1) * rows]
        at_expert = lax.broadcasted_iota(jnp.int32, total.shape, 0) == expert
        line = jnp.sum(jnp.where(at_expert, total, 0.0), axis=0, keepdims=True)
        square = (rows, rows)
        diagonal = lax.broadcasted_iota(jnp.int32, square, 0) == lax.broadcasted_iota(jnp.int32, square, 1)
        return jnp.sum(jnp.where(diagonal, jnp.broadcast_to(line, square), 0.0), axis=1, keepdims=True)

    by_core = (jnp.where(core == 0, own[2], near[2]), jnp.where(core == 0, near[2], own[2]))
    for c in range(2):
        weighted = result[c * rows : (c + 1) * rows] * weight(by_core[c])

        @pl.when(core == c)
        def _(weighted=weighted):
            own_out[...] = weighted

        @pl.when(core != c)
        def _(weighted=weighted):
            near_out[...] = weighted.astype(BF16)


def final_kernel(place, own, near, mine, shared, first_a, first_b, second_a, second_b, gain, out):
    core = place[0]
    rows, width = out.shape
    extra = own.shape[0] - 2 * rows
    half = width // 2
    cut = rows // 2
    at_rows = pl.ds(pl.multiple_of(core * (rows + extra), 16), rows)
    own_half, near_half = own[at_rows, :].astype(F32), near[at_rows, :].astype(F32)
    stream = jnp.concatenate(
        [jnp.where(core == 0, own_half, near_half), jnp.where(core == 0, near_half, own_half)], axis=1
    )
    base = stream + mine[...] + shared[...].astype(F32)
    sums = ((first_a, first_b), (second_a, second_b))
    for index, (a, b) in enumerate(sums):
        total = base[index * cut : (index + 1) * cut] + (a[...].astype(F32) + b[...].astype(F32))
        scale = lax.rsqrt(jnp.sum(total * total, axis=1, keepdims=True) / width + 1e-06)
        out[index * cut : (index + 1) * cut, :] = (total * scale * gain[...]).astype(BF16)


def body(
    attention,
    residual,
    out_weight,
    gate_weight,
    up_weight,
    down_weight,
    routes,
    router_scores,
    norm_gain,
):
    token_count, width = attention.shape
    half = width // 2
    groups = lax.axis_size("dp")
    peers = lax.axis_size("expert")
    chips = peers // 2
    far = chips // 2
    ring = ring_order(chips)
    forth = [(2 * ring[k] + c, 2 * ring[(k + 1) % chips] + c) for k in range(chips) for c in range(2)]
    back = [(b, a) for a, b in forth]
    across = [(e, e ^ 1) for e in range(peers)]
    group = lax.axis_index("dp")
    expert = lax.axis_index("expert")
    core = expert & 1
    place = jnp.stack([core, expert, group if groups == 2 else jnp.zeros_like(group)]).astype(jnp.int32)

    def swap(x):
        return lax.ppermute(x, "expert", across)

    def go(x):
        return lax.ppermute(x, "expert", forth)

    def come(x):
        return lax.ppermute(x, "expert", back)

    extra = -(-peers // 16) * 16
    block_rows = 2 * token_count + extra
    tokens, base = call(
        prepare_kernel,
        [
            jax.ShapeDtypeStruct((2 * token_count, width), BF16),
            jax.ShapeDtypeStruct((block_rows, half), BF16),
        ],
        place,
        attention,
        swap(attention),
        residual,
        swap(residual),
        routes.T,
        router_scores.T,
        name="prepare",
    )

    if groups == 2:
        flip = [(0, 1), (1, 0)]

        def columns(which):
            return lax.dynamic_slice(
                out_weight, (0, which * half), (out_weight.shape[0], half), allow_negative_indices=False
            )

        mine = jnp.concatenate([columns(core), swap(columns(1 - core))], axis=0)
        other = lax.ppermute(mine, "dp", flip)
        depth = out_weight.shape[0]
        blocks, layout = [mine, other], [(0, 0), (0, 1)]
        mine_f, mine_b = go(mine), come(mine)
        mine_f, mine_b, other, tokens, base = together(mine_f, mine_b, other, tokens, base)
        blocks += [mine_f, mine_b]
        layout += [(-1, 0), (1, 0)]
        other_f = other_b = other
        for step in range(1, far + 1):
            if step < far:
                mine_f = go(mine_f)
                blocks += [mine_f]
                layout += [(-step - 1, 0)]
                other_f = go(other_f)
                blocks += [other_f]
                layout += [(-step, 1)]
            if step < far - 1:
                mine_b = come(mine_b)
                blocks += [mine_b]
                layout += [(step + 1, 0)]
            other_b = come(other_b)
            blocks += [other_b]
            layout += [(step, 1)]
        layout = (chips, layout)
        gate, up = gate_weight[0], up_weight[0]
        other, gate_later, up_later = together(other, gate, up)
        gate_near, up_near = lax.ppermute(gate_later, "dp", flip), lax.ppermute(up_later, "dp", flip)
        *blocks, gate_near = together(*blocks, gate_near)
    else:
        blocks, layout = [lax.all_gather(out_weight, ("dp", "expert"), axis=0, tiled=True)], None
        gate_full = lax.all_gather(gate_weight, "dp", axis=1, tiled=True)[0]
        up_full = lax.all_gather(up_weight, "dp", axis=1, tiled=True)[0]
        gate, gate_near, up, up_near = gate_full[:half], gate_full[half:], up_full[:half], up_full[half:]

    stream = call(
        functools.partial(stream_kernel, layout),
        jax.ShapeDtypeStruct((block_rows, half), BF16),
        place,
        tokens,
        base,
        *blocks,
        scratch=[pltpu.VMEM((width, half), BF16)],
        flops=4 * token_count * width * half,
        name="stream",
    )

    def experts(*arrays):
        hidden = down_weight.shape[1]
        return call(
            functools.partial(expert_kernel, len(arrays) // 2),
            [
                jax.ShapeDtypeStruct((token_count, width), F32),
                jax.ShapeDtypeStruct((token_count, width), BF16),
            ],
            place,
            *arrays,
            gate,
            gate_near,
            up,
            up_near,
            down_weight[0],
            flops=4 * token_count * 3 * width * hidden,
            name="experts",
        )

    shared = {}
    stream_near = swap(stream)
    f = b = stream
    waiting = [(0, stream, stream_near)]
    results = {}
    for step in range(1, far + 1):
        if step < far:
            f, b = go(f), come(b)
        else:
            f, b = go(f[: token_count + extra]), come(b[token_count:])
        shared.update({offset: (own, swap(near)) for offset, (own, near) in results.items()})
        if step == 1:
            f, b, up_near = together(f, b, up_near)
            results = {}
        else:
            results = {offset: experts(*arrays) for offset, *arrays in waiting}
            waiting = []
            f, b, results, shared = together(f, b, results, shared)
        if step < far:
            waiting += [(-step, f, swap(f)), (step, b, swap(b))]
    shared.update({offset: (own, swap(near)) for offset, (own, near) in results.items()})

    cut = token_count // 2

    def term(offset, part):
        own, near = shared[offset]
        rows = slice(part * cut, (part + 1) * cut)
        return own[rows] + near[rows].astype(F32)

    ways = ((go, 1, 0), (come, -1, 1))

    def onward(received, left, flipped):
        return together(
            *(
                (term(sign * left, 1 - part if flipped else part) + x.astype(F32)).astype(BF16)
                for (_, sign, part), x in zip(ways, received)
            )
        )

    def send(pair):
        return [move(x) for (move, _, _), x in zip(ways, pair)]

    nearer = send(together(*(term(sign * (far - 1), 1 - part).astype(BF16) for _, sign, part in ways)))
    own, near = experts(f, b, swap(f), swap(b))
    pieces = 4
    near = [swap(near[i * token_count // pieces : (i + 1) * token_count // pieces]) for i in range(pieces)]
    shared[far] = (own, jnp.concatenate(near, axis=0))
    *farther, n0, n1 = together(*(term(far, part).astype(BF16) for _, _, part in ways), *nearer)
    nearer = [n0, n1]
    farther = send(farther)
    for left in range(far - 1, 0, -1):
        if left > 1:
            nearer = onward(nearer, left - 1, True)
            nearer_sent = send(nearer)
            farther = onward(farther, left, False)
            farther = together(*farther, *nearer)[:2]
            nearer = nearer_sent
        else:
            farther = onward(farther, left, False)
        farther = send(farther)

    return call(
        final_kernel,
        jax.ShapeDtypeStruct((token_count, width), BF16),
        place,
        stream,
        stream_near,
        *shared[0],
        farther[0],
        nearer[1],
        nearer[0],
        farther[1],
        norm_gain[None, :],
        name="final",
    )


def solution(mesh):
    in_specs = (
        P(("dp", "expert"), None),
        P(("dp", "expert"), None),
        P(("dp", "expert"), None),
        P("expert", "dp", None),
        P("expert", "dp", None),
        P("expert", None, None),
        P(("dp", "expert"), None),
        P(("dp", "expert"), None),
        P(),
    )
    out_specs = P(("dp", "expert"), None)
    return jax.shard_map(body, mesh=mesh, in_specs=in_specs, out_specs=out_specs, check_vma=False)
```

```python
import functools

import jax
import jax.numpy as jnp
from jax import lax
from jax.experimental import pallas as pl
from jax.experimental.pallas import tpu as pltpu
from jax.sharding import PartitionSpec as P

BF16 = jnp.bfloat16
F32 = jnp.float32
VMEM = pl.BlockSpec(memory_space=pltpu.VMEM)
SMEM = pl.BlockSpec(memory_space=pltpu.SMEM)
PIECES = 3
dot = functools.partial(jnp.dot, preferred_element_type=F32)


def ring_order(chips):
    return list(range(0, chips, 2)) + list(range(chips - 1, 0, -2))


def together(*arrays):
    return lax.optimization_barrier(arrays)


def call(kernel, out_shape, *args, scratch=(), flops=0, name=None):
    return pl.pallas_call(
        kernel,
        in_specs=[SMEM] + [VMEM] * (len(args) - 1),
        out_specs=jax.tree.map(lambda _: VMEM, out_shape),
        out_shape=out_shape,
        scratch_shapes=list(scratch),
        compiler_params=pltpu.CompilerParams(vmem_limit_bytes=32 * 1024 * 1024),
        cost_estimate=pl.CostEstimate(flops=flops, bytes_accessed=4 * 1024 * 1024, transcendentals=0),
        name=name,
    )(*args)


def prepare_kernel(peers, place, att, att_near, res, res_near, routes, scores, tokens, base, marks):
    core = place[0]
    rows, width = att.shape
    half = width // 2
    mine = pl.ds(pl.multiple_of(core * half, 128), half)
    tokens[:rows, :] = att[...]
    tokens[rows:, :] = att_near[...]
    base[:rows, :] = res[:, mine]
    base[rows:, :] = res_near[:, mine]
    combine = scores[...] / jnp.sum(scores[...], axis=0, keepdims=True)
    lanes = marks.shape[1]
    number = lax.broadcasted_iota(jnp.int32, (lanes, rows), 0)
    spread = jnp.zeros((lanes, rows), F32)
    for k in range(routes.shape[0]):
        left = combine[k : k + 1, :]
        for piece in range(PIECES):
            value = left.astype(BF16).astype(F32)
            spread = spread + jnp.where(routes[k : k + 1, :] + piece * peers == number, value, 0.0)
            left = left - value
    marks[...] = spread.T.astype(BF16)


def pack_kernel(place, gate, up, both):
    both[: gate.shape[0], :] = gate[...]
    both[gate.shape[0] :, :] = up[...]


def stream_kernel(layout, place, tokens, base, *refs):
    *blocks, own_out, near_out, full = refs
    core, expert, group = place[0], place[1], place[2]
    rows, width = tokens.shape[0] // 2, tokens.shape[1]
    half = width // 2
    if layout is None:
        full[...] = blocks[0][:, pl.ds(pl.multiple_of(core * half, 128), half)]
    else:
        chips, where = layout
        depth = blocks[0].shape[0] // 2
        pair = lax.shift_right_logical(expert, 1)
        down = (pair & 1) == 1
        at = jnp.where(down, chips - lax.shift_right_logical(pair + 1, 1), lax.shift_right_logical(pair, 1))
        for block, (offset, other) in zip(blocks, where, strict=True):
            spot = lax.rem(at + (offset + chips), chips)
            source = jnp.where(spot < chips // 2, 2 * spot, 2 * (chips - spot) - 1)
            of_group = group if other == 0 else 1 - group
            sides = (core, 1 - core)
            if block.shape[0] == depth:
                sides = sides[:1] if offset < 0 else sides[1:]
            for index, c in enumerate(sides):
                start = ((of_group * chips + source) * 2 + c) * depth
                full[pl.ds(pl.multiple_of(start, 16), depth), :] = block[index * depth : (index + 1) * depth, :]
    projected = dot(tokens[...], full[...])
    own_out[...] = (base[:rows, :].astype(F32) + projected[:rows]).astype(BF16)
    near_out[...] = (base[rows:, :].astype(F32) + projected[rows:]).astype(BF16)


def join_kernel(place, own, near, marks, *outs):
    core = place[0]
    half = own.shape[1]
    cut = outs[0].shape[0]
    for index, out in enumerate(outs):
        at = slice(index * cut, (index + 1) * cut)
        out[:, pl.ds(pl.multiple_of(core * half, 128), half)] = own[at, :]
        out[:, pl.ds(pl.multiple_of((1 - core) * half, 128), half)] = near[at, :]
        out[:, 2 * half :] = marks[at, :]


def expert_kernel(count, peers, place, *refs):
    blocks, refs = refs[:count], refs[count:]
    weights, outs = (refs[:3], refs[3:6]), refs[6:]
    expert, group = place[1], place[2]
    width = outs[0].shape[1]
    half = width // 2

    def columns(which):
        at = pl.ds(pl.multiple_of(which * half, 128), half)
        return jnp.concatenate([block[:, at] for block in blocks], axis=0)

    first, second = columns(group), columns(1 - group)
    marks = jnp.concatenate([block[:, width:] for block in blocks], axis=0).astype(F32)
    lane = lax.broadcasted_iota(jnp.int32, marks.shape, 1)
    total = None
    for index, (both_a, both_b, down) in enumerate(weights):
        gate_act = dot(first, both_a[:half, :]) + dot(second, both_b[:half, :])
        up_act = dot(first, both_a[half:, :]) + dot(second, both_b[half:, :])
        hidden = (jax.nn.silu(gate_act) * up_act).astype(BF16)
        number = expert if index == 0 else expert ^ 1
        named = lane == number
        for piece in range(1, PIECES):
            named = named | (lane == number + piece * peers)
        weighted = dot(hidden, down[...]) * jnp.sum(jnp.where(named, marks, 0.0), axis=1, keepdims=True)
        total = weighted if total is None else total + weighted
    start = 0
    for out in outs:
        out[...] = total[start : start + out.shape[0]]
        start += out.shape[0]


def final_kernel(place, *refs):
    *parts, gain, out = refs
    rows, width = out.shape
    cut = rows // 2
    for index in range(2):
        stream, mine, a, b = parts[index::2]
        total = stream[:, :width].astype(F32) + mine[...] + (a[...].astype(F32) + b[...].astype(F32))
        scale = lax.rsqrt(jnp.sum(total * total, axis=1, keepdims=True) / width + 1e-06)
        out[index * cut : (index + 1) * cut, :] = (total * scale * gain[...]).astype(BF16)


def body(
    attention,
    residual,
    out_weight,
    gate_weight,
    up_weight,
    down_weight,
    routes,
    router_scores,
    norm_gain,
):
    token_count, width = attention.shape
    half = width // 2
    groups = lax.axis_size("dp")
    peers = lax.axis_size("expert")
    chips = peers // 2
    far = chips // 2
    ring = ring_order(chips)
    forth = [(2 * ring[k] + c, 2 * ring[(k + 1) % chips] + c) for k in range(chips) for c in range(2)]
    back = [(b, a) for a, b in forth]
    across = [(e, e ^ 1) for e in range(peers)]
    group = lax.axis_index("dp")
    expert = lax.axis_index("expert")
    core = expert & 1
    place = jnp.stack([core, expert, group if groups == 2 else jnp.zeros_like(group)]).astype(jnp.int32)

    def swap(x):
        return lax.ppermute(x, "expert", across)

    def go(x):
        return lax.ppermute(x, "expert", forth)

    def come(x):
        return lax.ppermute(x, "expert", back)

    gate, up, down = gate_weight[0], up_weight[0], down_weight[0]
    hidden = gate.shape[1]
    lanes = -(-PIECES * peers // 128) * 128
    tokens, base, marks = call(
        functools.partial(prepare_kernel, peers),
        [
            jax.ShapeDtypeStruct((2 * token_count, width), BF16),
            jax.ShapeDtypeStruct((2 * token_count, half), BF16),
            jax.ShapeDtypeStruct((token_count, lanes), BF16),
        ],
        place,
        attention,
        swap(attention),
        residual,
        swap(residual),
        routes.T,
        router_scores.T,
        name="prepare",
    )
    down_near = swap(down)

    if groups == 2:
        flip = [(0, 1), (1, 0)]

        def columns(which):
            return lax.dynamic_slice(
                out_weight, (0, which * half), (out_weight.shape[0], half), allow_negative_indices=False
            )

        mine = jnp.concatenate([columns(core), swap(columns(1 - core))], axis=0)
        other = lax.ppermute(mine, "dp", flip)
        depth = out_weight.shape[0]
        blocks, layout = [mine, other], [(0, 0), (0, 1)]
        mine_f, mine_b = go(mine), come(mine)
        mine_f, mine_b, other, tokens, base, marks, down_near = together(
            mine_f, mine_b, other, tokens, base, marks, down_near
        )
        other, gate, up = together(other, gate, up)
        both = call(
            pack_kernel, jax.ShapeDtypeStruct((2 * gate.shape[0], hidden), BF16), place, gate, up, name="pack"
        )
        both_far = lax.ppermute(both, "dp", flip)
        both_near = swap(both)
        blocks += [mine_f, mine_b]
        layout += [(-1, 0), (1, 0)]
        other_f = other_b = other
        for step in range(1, far + 1):
            if step < far:
                mine_f = go(mine_f)
                if step == 1:
                    mine_f, both_near = together(mine_f, both_near)
                blocks += [mine_f]
                layout += [(-step - 1, 0)]
                other_f = go(other_f)
                blocks += [other_f]
                layout += [(-step, 1)]
            if step < far - 1:
                mine_b = come(mine_b)
                blocks += [mine_b]
                layout += [(step + 1, 0)]
            other_b = come(other_b)
            blocks += [other_b]
            layout += [(step, 1)]
        layout = (chips, layout)
    else:
        both = call(
            pack_kernel, jax.ShapeDtypeStruct((2 * gate.shape[0], hidden), BF16), place, gate, up, name="pack"
        )
        blocks, layout = [lax.all_gather(out_weight, ("dp", "expert"), axis=0, tiled=True)], None
        both = lax.all_gather(both, "dp", axis=0).reshape(groups, 2, -1, hidden).swapaxes(0, 1)
        both = both.reshape(2, 2, half, hidden).swapaxes(0, 1).reshape(2, 2 * half, hidden)
        both, both_far = both[0], both[1]
        both_near = swap(both)

    own_half, near_half = call(
        functools.partial(stream_kernel, layout),
        [jax.ShapeDtypeStruct((token_count, half), BF16)] * 2,
        place,
        tokens,
        base,
        *blocks,
        scratch=[pltpu.VMEM((width, half), BF16)],
        flops=4 * token_count * width * half,
        name="stream",
    )
    cut = token_count // 2
    stream = call(
        join_kernel,
        [jax.ShapeDtypeStruct((cut, width + lanes), BF16)] * 2,
        place,
        own_half,
        swap(near_half),
        marks,
        name="join",
    )

    def experts(*arrays):
        return call(
            functools.partial(expert_kernel, len(arrays), peers),
            [jax.ShapeDtypeStruct((array.shape[0], width), F32) for array in arrays],
            place,
            *arrays,
            *weights,
            flops=4 * sum(array.shape[0] for array in arrays) * 3 * width * hidden,
            name="experts",
        )

    terms = {}
    rows_at = {(0, 0): stream[0], (0, 1): stream[1]}

    def work(distance):
        offsets = [(offset, part) for offset in (-distance, distance) for part in range(2)]
        if distance == 1:
            offsets += [(0, 0), (0, 1)]
        return dict(zip(offsets, experts(*(rows_at[at] for at in offsets))))

    lead, rest = list(stream), list(stream[::-1])
    for step in range(1, far + 1):
        if step == far:
            lead, done = together(lead, work(far - 2))
            terms.update(done)
        lead = [go(lead[0]), come(lead[1])]
        if step == 1:
            _, both_far = together(lead, both_far)
            weights = (both, both_far, down, both_near, swap(both_far), down_near)
        if step == far:
            lead, done = together(lead, work(far - 1))
            terms.update(done)
            break
        rows_at[-step, 0], rows_at[step, 1] = lead
        if step > 2:
            rest, done = together(rest, work(step - 2))
            terms.update(done)
        rest = [go(rest[0]), come(rest[1])]
        rows_at[-step, 1], rows_at[step, 0] = rest

    def term(offset, part):
        return terms[offset, part]

    ways = ((go, 1, 0), (come, -1, 1))

    def onward(received, left, flipped):
        return together(
            *(
                (term(sign * left, 1 - part if flipped else part) + x.astype(F32)).astype(BF16)
                for (_, sign, part), x in zip(ways, received)
            )
        )

    def send(pair):
        return [move(x) for (move, _, _), x in zip(ways, pair)]

    nearer = send(together(*(term(sign * (far - 1), 1 - part).astype(BF16) for _, sign, part in ways)))
    farther = send(together(*(result.astype(BF16) for result in experts(*lead))))
    for left in range(far - 1, 0, -1):
        if left > 1:
            ready = onward(nearer, left - 1, True)
            farther = together(*onward(farther, left, False), *ready)[:2]
            if left == 2:
                ready = together(*ready, *farther)[:2]
            nearer = send(ready)
        else:
            farther = onward(farther, left, False)
        farther = send(farther)

    return call(
        final_kernel,
        jax.ShapeDtypeStruct((token_count, width), BF16),
        place,
        *stream,
        terms[0, 0],
        terms[0, 1],
        farther[0],
        nearer[0],
        nearer[1],
        farther[1],
        norm_gain[None, :],
        name="final",
    )


def solution(mesh):
    in_specs = (
        P(("dp", "expert"), None),
        P(("dp", "expert"), None),
        P(("dp", "expert"), None),
        P("expert", "dp", None),
        P("expert", "dp", None),
        P("expert", None, None),
        P(("dp", "expert"), None),
        P(("dp", "expert"), None),
        P(),
    )
    out_specs = P(("dp", "expert"), None)
    return jax.shard_map(body, mesh=mesh, in_specs=in_specs, out_specs=out_specs, check_vma=False)
```

```python
import functools

import jax
import jax.numpy as jnp
from jax import lax
from jax.experimental import pallas as pl
from jax.experimental.pallas import tpu as pltpu
from jax.sharding import PartitionSpec as P

BF16 = jnp.bfloat16
F32 = jnp.float32
VMEM = pl.BlockSpec(memory_space=pltpu.VMEM)
SMEM = pl.BlockSpec(memory_space=pltpu.SMEM)
PIECES = 3
dot = functools.partial(jnp.dot, preferred_element_type=F32)


def ring_order(chips):
    return list(range(0, chips, 2)) + list(range(chips - 1, 0, -2))


def together(*arrays):
    return lax.optimization_barrier(arrays)


def call(kernel, out_shape, *args, scratch=(), flops=0, name=None):
    return pl.pallas_call(
        kernel,
        in_specs=[SMEM] + [VMEM] * (len(args) - 1),
        out_specs=jax.tree.map(lambda _: VMEM, out_shape),
        out_shape=out_shape,
        scratch_shapes=list(scratch),
        compiler_params=pltpu.CompilerParams(vmem_limit_bytes=32 * 1024 * 1024),
        cost_estimate=pl.CostEstimate(flops=flops, bytes_accessed=4 * 1024 * 1024, transcendentals=0),
        name=name,
    )(*args)


def prepare_kernel(depth, peers, place, att, att_near, table, tokens, marks):
    core = place[0]
    rows, width = att.shape
    if depth:
        feature = lax.broadcasted_iota(jnp.int32, (width, tokens.shape[1]), 0)
        lane = lax.broadcasted_iota(jnp.int32, (width, tokens.shape[1]), 1)
        pick = (feature == 2 * lane - lax.rem(lane, depth) + core * depth).astype(BF16)
        tokens[:rows, :] = dot(att[...], pick).astype(BF16)
        tokens[rows:, :] = dot(att_near[...], pick).astype(BF16)
    chosen = table.shape[0] // 2
    scores = table[chosen:, :]
    combine = scores / jnp.sum(scores, axis=0, keepdims=True)
    lanes = marks.shape[1]
    number = lax.broadcasted_iota(jnp.int32, (lanes, rows), 0).astype(F32)
    spread = jnp.zeros((lanes, rows), F32)
    for k in range(chosen):
        left = combine[k : k + 1, :]
        for piece in range(PIECES):
            value = left.astype(BF16).astype(F32)
            spread = spread + jnp.where(table[k : k + 1, :] + float(piece * peers) == number, value, 0.0)
            left = left - value
    marks[...] = spread.T.astype(BF16)


def project_kernel(layout, place, tokens, *refs):
    *blocks, own_out, near_out, full = refs
    core, expert, group = place[0], place[1], place[2]
    rows = own_out.shape[0]
    chips, where = layout
    pair = lax.shift_right_logical(expert, 1)
    down = (pair & 1) == 1
    at = jnp.where(down, chips - lax.shift_right_logical(pair + 1, 1), lax.shift_right_logical(pair, 1))
    depth = blocks[0].shape[0]
    for block, (offset, other) in zip(blocks, where, strict=True):
        spot = lax.rem(at + (offset + chips), chips)
        source = jnp.where(spot < chips // 2, 2 * spot, 2 * (chips - spot) - 1)
        of_group = group if other == 0 else 1 - group
        full[pl.ds(pl.multiple_of((of_group * chips + source) * depth, 16), depth), :] = block[...]
    own_out[...] = dot(tokens[:rows, :], full[...])
    near_out[...] = dot(tokens[rows:, :], full[...])


def join_kernel(place, res, own, near, marks, *outs):
    width = res.shape[1]
    cut = outs[0].shape[0]
    for index, out in enumerate(outs):
        at = slice(index * cut, (index + 1) * cut)
        out[:, :width] = (res[at, :].astype(F32) + (own[at, :] + near[at, :])).astype(BF16)
        out[:, width:] = marks[at, :]


def expert_kernel(count, peers, place, *refs):
    blocks, refs = refs[:count], refs[count:]
    weights, outs = (refs[:3], refs[3:6]), refs[6:]
    expert, group = place[1], place[2]
    width = outs[0].shape[1]
    half = width // 2

    def columns(which):
        at = pl.ds(pl.multiple_of(which * half, 128), half)
        return jnp.concatenate([block[:, at] for block in blocks], axis=0)

    first, second = columns(group), columns(1 - group)
    marks = jnp.concatenate([block[:, width:] for block in blocks], axis=0).astype(F32)
    lane = lax.broadcasted_iota(jnp.int32, marks.shape, 1)
    total = None
    for index, (both_a, both_b, down) in enumerate(weights):
        gate_act = dot(first, both_a[:half, :]) + dot(second, both_b[:half, :])
        up_act = dot(first, both_a[half:, :]) + dot(second, both_b[half:, :])
        hidden = (jax.nn.silu(gate_act) * up_act).astype(BF16)
        number = expert if index == 0 else expert ^ 1
        named = lane == number
        for piece in range(1, PIECES):
            named = named | (lane == number + piece * peers)
        weighted = dot(hidden, down[...]) * jnp.sum(jnp.where(named, marks, 0.0), axis=1, keepdims=True)
        total = weighted if total is None else total + weighted
    start = 0
    for out in outs:
        out[...] = total[start : start + out.shape[0]]
        start += out.shape[0]


def final_kernel(place, *refs):
    *parts, gain, out = refs
    rows, width = out.shape
    cut = rows // 2
    for index in range(2):
        stream, mine, a, b = parts[index::2]
        total = stream[:, :width].astype(F32) + mine[...] + (a[...].astype(F32) + b[...].astype(F32))
        scale = lax.rsqrt(jnp.sum(total * total, axis=1, keepdims=True) / width + 1e-06)
        out[index * cut : (index + 1) * cut, :] = (total * scale * gain[...]).astype(BF16)


def body(
    attention,
    residual,
    out_weight,
    gate_weight,
    up_weight,
    down_weight,
    routes,
    router_scores,
    norm_gain,
):
    token_count, width = attention.shape
    half = width // 2
    groups = lax.axis_size("dp")
    peers = lax.axis_size("expert")
    chips = peers // 2
    far = chips // 2
    ring = ring_order(chips)
    forth = [(2 * ring[k] + c, 2 * ring[(k + 1) % chips] + c) for k in range(chips) for c in range(2)]
    back = [(b, a) for a, b in forth]
    across = [(e, e ^ 1) for e in range(peers)]
    group = lax.axis_index("dp")
    expert = lax.axis_index("expert")
    core = expert & 1
    place = jnp.stack([core, expert, group if groups == 2 else jnp.zeros_like(group)]).astype(jnp.int32)

    def swap(x):
        return lax.ppermute(x, "expert", across)

    def go(x):
        return lax.ppermute(x, "expert", forth)

    def come(x):
        return lax.ppermute(x, "expert", back)

    gate, up, down = gate_weight[0], up_weight[0], down_weight[0]
    hidden = gate.shape[1]
    lanes = -(-PIECES * peers // 128) * 128
    depth = out_weight.shape[0] if groups == 2 else 0
    tokens, marks = call(
        functools.partial(prepare_kernel, depth, peers),
        [
            jax.ShapeDtypeStruct((2 * token_count, half), BF16),
            jax.ShapeDtypeStruct((token_count, lanes), BF16),
        ],
        place,
        attention,
        swap(attention),
        jnp.concatenate([routes.T.astype(F32), router_scores.T], axis=0),
        name="prepare",
    )
    down_near = swap(down)

    if groups == 2:
        flip = [(0, 1), (1, 0)]
        mine, other = out_weight, lax.ppermute(out_weight, "dp", flip)
        blocks, layout = [mine, other], [(0, 0), (0, 1)]
        mine_f, mine_b = go(mine), come(mine)
        mine_f, mine_b, other, tokens, marks, down_near = together(
            mine_f, mine_b, other, tokens, marks, down_near
        )
        both = jnp.concatenate([gate, up], axis=0)
        other, both = together(other, both)
        both_far = lax.ppermute(both, "dp", flip)
        both_near = swap(both)
        blocks += [mine_f, mine_b]
        layout += [(-1, 0), (1, 0)]
        other_f = other_b = other
        for step in range(1, far + 1):
            if step < far:
                mine_f = go(mine_f)
                if step == 1:
                    mine_f, both_near = together(mine_f, both_near)
                blocks += [mine_f]
                layout += [(-step - 1, 0)]
                other_f = go(other_f)
                blocks += [other_f]
                layout += [(-step, 1)]
            if step < far - 1:
                mine_b = come(mine_b)
                blocks += [mine_b]
                layout += [(step + 1, 0)]
            other_b = come(other_b)
            blocks += [other_b]
            layout += [(step, 1)]
        layout = (chips, layout)
        own, near = call(
            functools.partial(project_kernel, layout),
            [jax.ShapeDtypeStruct((token_count, width), F32)] * 2,
            place,
            tokens,
            *blocks,
            scratch=[pltpu.VMEM((half, width), BF16)],
            flops=4 * token_count * width * half,
            name="project",
        )
        near = swap(near)
    else:
        both = jnp.concatenate([gate, up], axis=0)
        both = lax.all_gather(both, "dp", axis=0).reshape(groups, 2, -1, hidden).swapaxes(0, 1)
        both = both.reshape(2, 2, half, hidden).swapaxes(0, 1).reshape(2, 2 * half, hidden)
        both, both_far = both[0], both[1]
        both_near = swap(both)
        full_weight = lax.all_gather(out_weight, ("dp", "expert"), axis=0, tiled=True)
        own = jnp.dot(attention, full_weight, preferred_element_type=F32)
        near = jnp.zeros_like(own)

    cut = token_count // 2
    stream = call(
        join_kernel,
        [jax.ShapeDtypeStruct((cut, width + lanes), BF16)] * 2,
        place,
        residual,
        own,
        near,
        marks,
        name="stream",
    )

    def experts(*arrays):
        return call(
            functools.partial(expert_kernel, len(arrays), peers),
            [jax.ShapeDtypeStruct((array.shape[0], width), F32) for array in arrays],
            place,
            *arrays,
            *weights,
            flops=4 * sum(array.shape[0] for array in arrays) * 3 * width * hidden,
            name="experts",
        )

    terms = {}
    rows_at = {(0, 0): stream[0], (0, 1): stream[1]}

    def work(distance):
        offsets = [(offset, part) for offset in (-distance, distance) for part in range(2)]
        if distance == 1:
            offsets += [(0, 0), (0, 1)]
        return dict(zip(offsets, experts(*(rows_at[at] for at in offsets))))

    lead, rest = list(stream), list(stream[::-1])
    for step in range(1, far + 1):
        if step == far:
            lead, done = together(lead, work(far - 2))
            terms.update(done)
        lead = [go(lead[0]), come(lead[1])]
        if step == 1:
            _, both_far = together(lead, both_far)
            weights = (both, both_far, down, both_near, swap(both_far), down_near)
        if step == far:
            lead, done = together(lead, work(far - 1))
            terms.update(done)
            break
        rows_at[-step, 0], rows_at[step, 1] = lead
        if step > 2:
            rest, done = together(rest, work(step - 2))
            terms.update(done)
        rest = [go(rest[0]), come(rest[1])]
        rows_at[-step, 1], rows_at[step, 0] = rest

    def term(offset, part):
        return terms[offset, part]

    ways = ((go, 1, 0), (come, -1, 1))

    def onward(received, left, flipped):
        return together(
            *(
                (term(sign * left, 1 - part if flipped else part) + x.astype(F32)).astype(BF16)
                for (_, sign, part), x in zip(ways, received)
            )
        )

    def send(pair):
        return [move(x) for (move, _, _), x in zip(ways, pair)]

    nearer = send(together(*(term(sign * (far - 1), 1 - part).astype(BF16) for _, sign, part in ways)))
    farther = send(together(*(result.astype(BF16) for result in experts(*lead))))
    for left in range(far - 1, 0, -1):
        if left > 1:
            ready = onward(nearer, left - 1, True)
            farther = together(*onward(farther, left, False), *ready)[:2]
            if left == 2:
                ready = together(*ready, *farther)[:2]
            nearer = send(ready)
        else:
            farther = onward(farther, left, False)
        farther = send(farther)

    return call(
        final_kernel,
        jax.ShapeDtypeStruct((token_count, width), BF16),
        place,
        *stream,
        terms[0, 0],
        terms[0, 1],
        farther[0],
        nearer[0],
        nearer[1],
        farther[1],
        norm_gain[None, :],
        name="final",
    )


def solution(mesh):
    in_specs = (
        P(("dp", "expert"), None),
        P(("dp", "expert"), None),
        P(("dp", "expert"), None),
        P("expert", "dp", None),
        P("expert", "dp", None),
        P("expert", None, None),
        P(("dp", "expert"), None),
        P(("dp", "expert"), None),
        P(),
    )
    out_specs = P(("dp", "expert"), None)
    return jax.shard_map(body, mesh=mesh, in_specs=in_specs, out_specs=out_specs, check_vma=False)
```

```python
import functools

import jax
import jax.numpy as jnp
from jax import lax
from jax.experimental import pallas as pl
from jax.experimental.pallas import tpu as pltpu
from jax.sharding import PartitionSpec as P

BF16 = jnp.bfloat16
F32 = jnp.float32
VMEM = pl.BlockSpec(memory_space=pltpu.VMEM)
SMEM = pl.BlockSpec(memory_space=pltpu.SMEM)
PIECES = 3
dot = functools.partial(jnp.dot, preferred_element_type=F32)


def ring_order(chips):
    return list(range(0, chips, 2)) + list(range(chips - 1, 0, -2))


def together(*arrays):
    return lax.optimization_barrier(arrays)


def call(kernel, out_shape, *args, scratch=(), flops=0, name=None):
    return pl.pallas_call(
        kernel,
        in_specs=[SMEM] + [VMEM] * (len(args) - 1),
        out_specs=jax.tree.map(lambda _: VMEM, out_shape),
        out_shape=out_shape,
        scratch_shapes=list(scratch),
        compiler_params=pltpu.CompilerParams(vmem_limit_bytes=32 * 1024 * 1024),
        cost_estimate=pl.CostEstimate(flops=flops, bytes_accessed=4 * 1024 * 1024, transcendentals=0),
        name=name,
    )(*args)


def prepare_kernel(depth, peers, place, att, att_near, table, tokens, marks):
    core = place[0]
    rows, width = att.shape
    if depth:
        feature = lax.broadcasted_iota(jnp.int32, (width, tokens.shape[1]), 0)
        lane = lax.broadcasted_iota(jnp.int32, (width, tokens.shape[1]), 1)
        pick = (feature == 2 * lane - lax.rem(lane, depth) + core * depth).astype(BF16)
        tokens[:rows, :] = dot(att[...], pick).astype(BF16)
        tokens[rows:, :] = dot(att_near[...], pick).astype(BF16)
    chosen = table.shape[0] // 2
    scores = table[chosen:, :]
    combine = scores / jnp.sum(scores, axis=0, keepdims=True)
    lanes = marks.shape[1]
    number = lax.broadcasted_iota(jnp.int32, (lanes, rows), 0).astype(F32)
    spread = jnp.zeros((lanes, rows), F32)
    for k in range(chosen):
        left = combine[k : k + 1, :]
        for piece in range(PIECES):
            value = left.astype(BF16).astype(F32)
            spread = spread + jnp.where(table[k : k + 1, :] + float(piece * peers) == number, value, 0.0)
            left = left - value
    marks[...] = spread.T.astype(BF16)


def project_kernel(layout, place, tokens, *refs):
    *blocks, own_out, near_out, full = refs
    core, expert, group = place[0], place[1], place[2]
    rows = own_out.shape[0]
    chips, where = layout
    pair = lax.shift_right_logical(expert, 1)
    down = (pair & 1) == 1
    at = jnp.where(down, chips - lax.shift_right_logical(pair + 1, 1), lax.shift_right_logical(pair, 1))
    depth = blocks[0].shape[0]
    for block, (offset, other) in zip(blocks, where, strict=True):
        spot = lax.rem(at + (offset + chips), chips)
        source = jnp.where(spot < chips // 2, 2 * spot, 2 * (chips - spot) - 1)
        of_group = group if other == 0 else 1 - group
        full[pl.ds(pl.multiple_of((of_group * chips + source) * depth, 16), depth), :] = block[...]
    own_out[...] = dot(tokens[:rows, :], full[...])
    near_out[...] = dot(tokens[rows:, :], full[...])


def join_kernel(place, res, own, near, marks, *outs):
    width = res.shape[1]
    cut = outs[0].shape[0]
    for index, out in enumerate(outs):
        at = slice(index * cut, (index + 1) * cut)
        out[:, :width] = (res[at, :].astype(F32) + (own[at, :] + near[at, :])).astype(BF16)
        out[:, width:] = marks[at, :]


def expert_kernel(count, peers, place, *refs):
    blocks, refs = refs[:count], refs[count:]
    weights, outs = (refs[:3], refs[3:6]), refs[6:]
    expert, group = place[1], place[2]
    width = outs[0].shape[1]
    half = width // 2

    def columns(which):
        at = pl.ds(pl.multiple_of(which * half, 128), half)
        return jnp.concatenate([block[:, at] for block in blocks], axis=0)

    first, second = columns(group), columns(1 - group)
    marks = jnp.concatenate([block[:, width:] for block in blocks], axis=0).astype(F32)
    lane = lax.broadcasted_iota(jnp.int32, marks.shape, 1)
    total = None
    for index, (both_a, both_b, down) in enumerate(weights):
        gate_act = dot(first, both_a[:half, :]) + dot(second, both_b[:half, :])
        up_act = dot(first, both_a[half:, :]) + dot(second, both_b[half:, :])
        hidden = (jax.nn.silu(gate_act) * up_act).astype(BF16)
        number = expert if index == 0 else expert ^ 1
        named = lane == number
        for piece in range(1, PIECES):
            named = named | (lane == number + piece * peers)
        weighted = dot(hidden, down[...]) * jnp.sum(jnp.where(named, marks, 0.0), axis=1, keepdims=True)
        total = weighted if total is None else total + weighted
    start = 0
    for out in outs:
        out[...] = total[start : start + out.shape[0]]
        start += out.shape[0]


def final_kernel(place, *refs):
    *parts, gain, out = refs
    rows, width = out.shape
    cut = rows // 2
    for index in range(2):
        stream, mine, a, b = parts[index::2]
        total = stream[:, :width].astype(F32) + mine[...] + (a[...].astype(F32) + b[...].astype(F32))
        scale = lax.rsqrt(jnp.sum(total * total, axis=1, keepdims=True) / width + 1e-06)
        out[index * cut : (index + 1) * cut, :] = (total * scale * gain[...]).astype(BF16)


def body(
    attention,
    residual,
    out_weight,
    gate_weight,
    up_weight,
    down_weight,
    routes,
    router_scores,
    norm_gain,
):
    token_count, width = attention.shape
    half = width // 2
    groups = lax.axis_size("dp")
    peers = lax.axis_size("expert")
    chips = peers // 2
    far = chips // 2
    ring = ring_order(chips)
    forth = [(2 * ring[k] + c, 2 * ring[(k + 1) % chips] + c) for k in range(chips) for c in range(2)]
    back = [(b, a) for a, b in forth]
    across = [(e, e ^ 1) for e in range(peers)]
    group = lax.axis_index("dp")
    expert = lax.axis_index("expert")
    core = expert & 1
    place = jnp.stack([core, expert, group if groups == 2 else jnp.zeros_like(group)]).astype(jnp.int32)

    def swap(x):
        return lax.ppermute(x, "expert", across)

    def go(x):
        return lax.ppermute(x, "expert", forth)

    def come(x):
        return lax.ppermute(x, "expert", back)

    gate, up, down = gate_weight[0], up_weight[0], down_weight[0]
    hidden = gate.shape[1]
    lanes = -(-PIECES * peers // 128) * 128
    depth = out_weight.shape[0] if groups == 2 else 0
    tokens, marks = call(
        functools.partial(prepare_kernel, depth, peers),
        [
            jax.ShapeDtypeStruct((2 * token_count, half), BF16),
            jax.ShapeDtypeStruct((token_count, lanes), BF16),
        ],
        place,
        attention,
        swap(attention),
        jnp.concatenate([routes.T.astype(F32), router_scores.T], axis=0),
        name="prepare",
    )
    down_near = swap(down)

    if groups == 2:
        flip = [(0, 1), (1, 0)]
        mine, other = out_weight, lax.ppermute(out_weight, "dp", flip)
        blocks, layout = [mine, other], [(0, 0), (0, 1)]
        mine_f, mine_b = go(mine), come(mine)
        mine_f, mine_b, other, tokens, marks, down_near = together(
            mine_f, mine_b, other, tokens, marks, down_near
        )
        both = jnp.concatenate([gate, up], axis=0)
        other, both = together(other, both)
        both_far = lax.ppermute(both, "dp", flip)
        both_near = swap(both)
        blocks += [mine_f, mine_b]
        layout += [(-1, 0), (1, 0)]
        other_f = other_b = other
        for step in range(1, far + 1):
            if step < far:
                mine_f = go(mine_f)
                if step == 1:
                    mine_f, both_near = together(mine_f, both_near)
                blocks += [mine_f]
                layout += [(-step - 1, 0)]
                other_f = go(other_f)
                blocks += [other_f]
                layout += [(-step, 1)]
            if step < far - 1:
                mine_b = come(mine_b)
                blocks += [mine_b]
                layout += [(step + 1, 0)]
            other_b = come(other_b)
            blocks += [other_b]
            layout += [(step, 1)]
        layout = (chips, layout)
        own, near = call(
            functools.partial(project_kernel, layout),
            [jax.ShapeDtypeStruct((token_count, width), F32)] * 2,
            place,
            tokens,
            *blocks,
            scratch=[pltpu.VMEM((half, width), BF16)],
            flops=4 * token_count * width * half,
            name="project",
        )
        near = swap(near)
    else:
        both = jnp.concatenate([gate, up], axis=0)
        both = lax.all_gather(both, "dp", axis=0).reshape(groups, 2, -1, hidden).swapaxes(0, 1)
        both = both.reshape(2, 2, half, hidden).swapaxes(0, 1).reshape(2, 2 * half, hidden)
        both, both_far = both[0], both[1]
        both_near = swap(both)
        full_weight = lax.all_gather(out_weight, ("dp", "expert"), axis=0, tiled=True)
        own = jnp.dot(attention, full_weight, preferred_element_type=F32)
        near = jnp.zeros_like(own)

    cut = token_count // 2
    stream = call(
        join_kernel,
        [jax.ShapeDtypeStruct((cut, width + lanes), BF16)] * 2,
        place,
        residual,
        own,
        near,
        marks,
        name="stream",
    )

    def experts(*arrays):
        return call(
            functools.partial(expert_kernel, len(arrays), peers),
            [jax.ShapeDtypeStruct((array.shape[0], width), F32) for array in arrays],
            place,
            *arrays,
            *weights,
            flops=4 * sum(array.shape[0] for array in arrays) * 3 * width * hidden,
            name="experts",
        )

    terms = {}
    rows_at = {(0, 0): stream[0], (0, 1): stream[1]}

    def work(distance):
        offsets = [(offset, part) for offset in (-distance, distance) for part in range(2)]
        if distance == 1:
            offsets += [(0, 0), (0, 1)]
        return dict(zip(offsets, experts(*(rows_at[at] for at in offsets))))

    lead, rest = list(stream), list(stream[::-1])
    for step in range(1, far + 1):
        if step == far:
            lead, done = together(lead, work(far - 2))
            terms.update(done)
        lead = [go(lead[0]), come(lead[1])]
        if step == 1:
            _, both_far = together(lead, both_far)
            weights = (both, both_far, down, both_near, swap(both_far), down_near)
        if step == far:
            terms.update(work(far - 1))
            break
        rows_at[-step, 0], rows_at[step, 1] = lead
        if step > 2:
            rest, done = together(rest, work(step - 2))
            terms.update(done)
        rest = [go(rest[0]), come(rest[1])]
        rows_at[-step, 1], rows_at[step, 0] = rest

    def term(offset, part):
        return terms[offset, part]

    ways = ((go, 1, 0), (come, -1, 1))

    def onward(received, left, flipped):
        return together(
            *(
                (term(sign * left, 1 - part if flipped else part) + x.astype(F32)).astype(BF16)
                for (_, sign, part), x in zip(ways, received)
            )
        )

    def send(pair):
        return [move(x) for (move, _, _), x in zip(ways, pair)]

    nearer = send(together(*(term(sign * (far - 1), 1 - part).astype(BF16) for _, sign, part in ways)))
    farther = send(together(*(result.astype(BF16) for result in experts(*lead))))
    for left in range(far - 1, 0, -1):
        if left > 1:
            ready = onward(nearer, left - 1, True)
            farther = together(*onward(farther, left, False), *ready)[:2]
            if left == 2:
                ready = together(*ready, *farther)[:2]
            nearer = send(ready)
        else:
            farther = onward(farther, left, False)
        farther = send(farther)

    return call(
        final_kernel,
        jax.ShapeDtypeStruct((token_count, width), BF16),
        place,
        *stream,
        terms[0, 0],
        terms[0, 1],
        farther[0],
        nearer[0],
        nearer[1],
        farther[1],
        norm_gain[None, :],
        name="final",
    )


def solution(mesh):
    in_specs = (
        P(("dp", "expert"), None),
        P(("dp", "expert"), None),
        P(("dp", "expert"), None),
        P("expert", "dp", None),
        P("expert", "dp", None),
        P("expert", None, None),
        P(("dp", "expert"), None),
        P(("dp", "expert"), None),
        P(),
    )
    out_specs = P(("dp", "expert"), None)
    return jax.shard_map(body, mesh=mesh, in_specs=in_specs, out_specs=out_specs, check_vma=False)
```

```python
import functools

import jax
import jax.numpy as jnp
from jax import lax
from jax.experimental import pallas as pl
from jax.experimental.pallas import tpu as pltpu
from jax.sharding import PartitionSpec as P

BF16 = jnp.bfloat16
F32 = jnp.float32
VMEM = pl.BlockSpec(memory_space=pltpu.VMEM)
SMEM = pl.BlockSpec(memory_space=pltpu.SMEM)
PIECES = 3
dot = functools.partial(jnp.dot, preferred_element_type=F32)


def ring_order(chips):
    return list(range(0, chips, 2)) + list(range(chips - 1, 0, -2))


def together(*arrays):
    return lax.optimization_barrier(arrays)


def call(kernel, out_shape, *args, scratch=(), flops=0, name=None):
    return pl.pallas_call(
        kernel,
        in_specs=[SMEM] + [VMEM] * (len(args) - 1),
        out_specs=jax.tree.map(lambda _: VMEM, out_shape),
        out_shape=out_shape,
        scratch_shapes=list(scratch),
        compiler_params=pltpu.CompilerParams(vmem_limit_bytes=32 * 1024 * 1024),
        cost_estimate=pl.CostEstimate(flops=flops, bytes_accessed=4 * 1024 * 1024, transcendentals=0),
        name=name,
    )(*args)


def prepare_kernel(depth, peers, place, att, att_near, table, tokens, marks):
    core = place[0]
    rows, width = att.shape
    if depth:
        feature = lax.broadcasted_iota(jnp.int32, (width, tokens.shape[1]), 0)
        lane = lax.broadcasted_iota(jnp.int32, (width, tokens.shape[1]), 1)
        pick = (feature == 2 * lane - lax.rem(lane, depth) + core * depth).astype(BF16)
        tokens[:rows, :] = dot(att[...], pick).astype(BF16)
        tokens[rows:, :] = dot(att_near[...], pick).astype(BF16)
    chosen = table.shape[0] // 2
    scores = table[chosen:, :]
    combine = scores / jnp.sum(scores, axis=0, keepdims=True)
    lanes = marks.shape[1]
    number = lax.broadcasted_iota(jnp.int32, (lanes, rows), 0).astype(F32)
    spread = jnp.zeros((lanes, rows), F32)
    for k in range(chosen):
        left = combine[k : k + 1, :]
        for piece in range(PIECES):
            value = left.astype(BF16).astype(F32)
            spread = spread + jnp.where(table[k : k + 1, :] + float(piece * peers) == number, value, 0.0)
            left = left - value
    marks[...] = spread.T.astype(BF16)


def project_kernel(layout, place, tokens, *refs):
    *blocks, near_out, full = refs
    core, expert, group = place[0], place[1], place[2]
    rows = near_out.shape[0]
    chips, where = layout
    pair = lax.shift_right_logical(expert, 1)
    down = (pair & 1) == 1
    at = jnp.where(down, chips - lax.shift_right_logical(pair + 1, 1), lax.shift_right_logical(pair, 1))
    depth = blocks[0].shape[0]
    for block, (offset, other) in zip(blocks, where, strict=True):
        spot = lax.rem(at + (offset + chips), chips)
        source = jnp.where(spot < chips // 2, 2 * spot, 2 * (chips - spot) - 1)
        of_group = group if other == 0 else 1 - group
        full[pl.ds(pl.multiple_of((of_group * chips + source) * depth, 16), depth), :] = block[...]
    near_out[...] = dot(tokens[rows:, :], full[...])


def own_kernel(place, tokens, full, own):
    own[...] = dot(tokens[: own.shape[0], :], full[...])


def join_kernel(place, res, own, near, marks, *outs):
    width = res.shape[1]
    cut = outs[0].shape[0]
    for index, out in enumerate(outs):
        at = slice(index * cut, (index + 1) * cut)
        out[:, :width] = (res[at, :].astype(F32) + (own[at, :] + near[at, :])).astype(BF16)
        out[:, width:] = marks[at, :]


def expert_kernel(count, peers, place, *refs):
    blocks, refs = refs[:count], refs[count:]
    weights, outs = (refs[:3], refs[3:6]), refs[6:]
    expert, group = place[1], place[2]
    width = outs[0].shape[1]
    half = width // 2

    def columns(which):
        at = pl.ds(pl.multiple_of(which * half, 128), half)
        return jnp.concatenate([block[:, at] for block in blocks], axis=0)

    first, second = columns(group), columns(1 - group)
    marks = jnp.concatenate([block[:, width:] for block in blocks], axis=0).astype(F32)
    lane = lax.broadcasted_iota(jnp.int32, marks.shape, 1)
    total = None
    for index, (both_a, both_b, down) in enumerate(weights):
        gate_act = dot(first, both_a[:half, :]) + dot(second, both_b[:half, :])
        up_act = dot(first, both_a[half:, :]) + dot(second, both_b[half:, :])
        hidden = (jax.nn.silu(gate_act) * up_act).astype(BF16)
        number = expert if index == 0 else expert ^ 1
        named = lane == number
        for piece in range(1, PIECES):
            named = named | (lane == number + piece * peers)
        weighted = dot(hidden, down[...]) * jnp.sum(jnp.where(named, marks, 0.0), axis=1, keepdims=True)
        total = weighted if total is None else total + weighted
    start = 0
    for out in outs:
        out[...] = total[start : start + out.shape[0]]
        start += out.shape[0]


def final_kernel(place, *refs):
    *parts, gain, out = refs
    rows, width = out.shape
    cut = rows // 2
    for index in range(2):
        stream, mine, a, b = parts[index::2]
        total = stream[:, :width].astype(F32) + mine[...] + (a[...].astype(F32) + b[...].astype(F32))
        scale = lax.rsqrt(jnp.sum(total * total, axis=1, keepdims=True) / width + 1e-06)
        out[index * cut : (index + 1) * cut, :] = (total * scale * gain[...]).astype(BF16)


def body(
    attention,
    residual,
    out_weight,
    gate_weight,
    up_weight,
    down_weight,
    routes,
    router_scores,
    norm_gain,
):
    token_count, width = attention.shape
    half = width // 2
    groups = lax.axis_size("dp")
    peers = lax.axis_size("expert")
    chips = peers // 2
    far = chips // 2
    ring = ring_order(chips)
    forth = [(2 * ring[k] + c, 2 * ring[(k + 1) % chips] + c) for k in range(chips) for c in range(2)]
    back = [(b, a) for a, b in forth]
    across = [(e, e ^ 1) for e in range(peers)]
    group = lax.axis_index("dp")
    expert = lax.axis_index("expert")
    core = expert & 1
    place = jnp.stack([core, expert, group if groups == 2 else jnp.zeros_like(group)]).astype(jnp.int32)

    def swap(x):
        return lax.ppermute(x, "expert", across)

    def go(x):
        return lax.ppermute(x, "expert", forth)

    def come(x):
        return lax.ppermute(x, "expert", back)

    gate, up, down = gate_weight[0], up_weight[0], down_weight[0]
    hidden = gate.shape[1]
    lanes = -(-PIECES * peers // 128) * 128
    depth = out_weight.shape[0] if groups == 2 else 0
    tokens, marks = call(
        functools.partial(prepare_kernel, depth, peers),
        [
            jax.ShapeDtypeStruct((2 * token_count, half), BF16),
            jax.ShapeDtypeStruct((token_count, lanes), BF16),
        ],
        place,
        attention,
        swap(attention),
        jnp.concatenate([routes.T.astype(F32), router_scores.T], axis=0),
        name="prepare",
    )
    down_near = swap(down)

    if groups == 2:
        flip = [(0, 1), (1, 0)]
        mine, other = out_weight, lax.ppermute(out_weight, "dp", flip)
        blocks, layout = [mine, other], [(0, 0), (0, 1)]
        mine_f, mine_b = go(mine), come(mine)
        mine_f, mine_b, other, tokens, marks, down_near = together(
            mine_f, mine_b, other, tokens, marks, down_near
        )
        both = jnp.concatenate([gate, up], axis=0)
        other, both = together(other, both)
        both_far = lax.ppermute(both, "dp", flip)
        both_near = swap(both)
        blocks += [mine_f, mine_b]
        layout += [(-1, 0), (1, 0)]
        other_f = other_b = other
        for step in range(1, far + 1):
            if step < far:
                mine_f = go(mine_f)
                if step == 1:
                    mine_f, both_near = together(mine_f, both_near)
                blocks += [mine_f]
                layout += [(-step - 1, 0)]
                other_f = go(other_f)
                blocks += [other_f]
                layout += [(-step, 1)]
            if step < far - 1:
                mine_b = come(mine_b)
                blocks += [mine_b]
                layout += [(step + 1, 0)]
            other_b = come(other_b)
            blocks += [other_b]
            layout += [(step, 1)]
        layout = (chips, layout)
        near, full = call(
            functools.partial(project_kernel, layout),
            [
                jax.ShapeDtypeStruct((token_count, width), F32),
                jax.ShapeDtypeStruct((half, width), BF16),
            ],
            place,
            tokens,
            *blocks,
            flops=2 * token_count * width * half,
            name="project",
        )
        own = call(
            own_kernel,
            jax.ShapeDtypeStruct((token_count, width), F32),
            place,
            tokens,
            full,
            flops=2 * token_count * width * half,
            name="own",
        )
        near = swap(near)
    else:
        both = jnp.concatenate([gate, up], axis=0)
        both = lax.all_gather(both, "dp", axis=0).reshape(groups, 2, -1, hidden).swapaxes(0, 1)
        both = both.reshape(2, 2, half, hidden).swapaxes(0, 1).reshape(2, 2 * half, hidden)
        both, both_far = both[0], both[1]
        both_near = swap(both)
        full_weight = lax.all_gather(out_weight, ("dp", "expert"), axis=0, tiled=True)
        own = jnp.dot(attention, full_weight, preferred_element_type=F32)
        near = jnp.zeros_like(own)

    cut = token_count // 2
    stream = call(
        join_kernel,
        [jax.ShapeDtypeStruct((cut, width + lanes), BF16)] * 2,
        place,
        residual,
        own,
        near,
        marks,
        name="stream",
    )

    def experts(*arrays):
        return call(
            functools.partial(expert_kernel, len(arrays), peers),
            [jax.ShapeDtypeStruct((array.shape[0], width), F32) for array in arrays],
            place,
            *arrays,
            *weights,
            flops=4 * sum(array.shape[0] for array in arrays) * 3 * width * hidden,
            name="experts",
        )

    terms = {}
    rows_at = {(0, 0): stream[0], (0, 1): stream[1]}

    def work(distance):
        offsets = [(offset, part) for offset in (-distance, distance) for part in range(2)]
        if distance == 1:
            offsets += [(0, 0), (0, 1)]
        return dict(zip(offsets, experts(*(rows_at[at] for at in offsets))))

    lead, rest = list(stream), list(stream[::-1])
    for step in range(1, far + 1):
        if step == far:
            lead, done = together(lead, work(far - 2))
            terms.update(done)
        lead = [go(lead[0]), come(lead[1])]
        if step == 1:
            _, both_far = together(lead, both_far)
            weights = (both, both_far, down, both_near, swap(both_far), down_near)
        if step == far:
            terms.update(work(far - 1))
            break
        rows_at[-step, 0], rows_at[step, 1] = lead
        if step > 2:
            rest, done = together(rest, work(step - 2))
            terms.update(done)
        rest = [go(rest[0]), come(rest[1])]
        rows_at[-step, 1], rows_at[step, 0] = rest

    def term(offset, part):
        return terms[offset, part]

    ways = ((go, 1, 0), (come, -1, 1))

    def onward(received, left, flipped):
        return together(
            *(
                (term(sign * left, 1 - part if flipped else part) + x.astype(F32)).astype(BF16)
                for (_, sign, part), x in zip(ways, received)
            )
        )

    def send(pair):
        return [move(x) for (move, _, _), x in zip(ways, pair)]

    nearer = send(together(*(term(sign * (far - 1), 1 - part).astype(BF16) for _, sign, part in ways)))
    farther = send(together(*(result.astype(BF16) for result in experts(*lead))))
    for left in range(far - 1, 0, -1):
        if left > 1:
            ready = onward(nearer, left - 1, True)
            farther = together(*onward(farther, left, False), *ready)[:2]
            if left == 2:
                ready = together(*ready, *farther)[:2]
            nearer = send(ready)
        else:
            farther = onward(farther, left, False)
        farther = send(farther)

    return call(
        final_kernel,
        jax.ShapeDtypeStruct((token_count, width), BF16),
        place,
        *stream,
        terms[0, 0],
        terms[0, 1],
        farther[0],
        nearer[0],
        nearer[1],
        farther[1],
        norm_gain[None, :],
        name="final",
    )


def solution(mesh):
    in_specs = (
        P(("dp", "expert"), None),
        P(("dp", "expert"), None),
        P(("dp", "expert"), None),
        P("expert", "dp", None),
        P("expert", "dp", None),
        P("expert", None, None),
        P(("dp", "expert"), None),
        P(("dp", "expert"), None),
        P(),
    )
    out_specs = P(("dp", "expert"), None)
    return jax.shard_map(body, mesh=mesh, in_specs=in_specs, out_specs=out_specs, check_vma=False)
```
